128 devices in a mesh: dap: 32 (over z, x, core), rep: 4 (over y).
Axes of the slice: x: 4, y: 4, z: 4, core: 2. Of those that a mesh axis runs over, the one named last changes fastest.
Arguments:
- alignment_features: bfloat16 [256, 2048, 256], P('dap', 'rep'), may hold values from -6 to 6
- presence_indicator: bfloat16 [256, 2048], P('dap', 'rep'), may hold values from 0 to 1, as said below
- genuine_position_indicator: int32 [2048], replicated, may hold values from 0 to 1, as said below
- standardizer_scale: float32 [256], replicated, may hold values from 0.1 to 1.9
- standardizer_offset: float32 [256], replicated, may hold values from -3 to 3
- first_factor_matrix: bfloat16 [256, 32], replicated, may hold values from -0.375 to 0.375
- first_factor_offset: float32 [32], replicated, may hold values from -3 to 3
- second_factor_matrix: bfloat16 [256, 32], replicated, may hold values from -0.375 to 0.375
- second_factor_offset: float32 [32], replicated, may hold values from -3 to 3
- final_projection_matrix: bfloat16 [1024, 128], replicated, may hold values from -1.5 to 1.5
- final_projection_offset: float32 [128], replicated, may hold values from -3 to 3
Outputs:
- pair_update: bfloat16 [2048, 2048, 128], P('dap', 'rep')
The draws below stay inside these ranges and needn't reach their ends.
Inputs may be any that keep to these rules, and one draw needn't show every extreme that they name: `genuine_position_indicator`: 1 for the first residues up to a drawn length and 0 after it; some residues are padding. `presence_indicator`: 0 for absent entries, a real weight otherwise.
All inputs are finite; a program needn't handle non-finite values.
Results may differ from the reference program's by a relative error of at most 0.0054.
Values may be sent and summed in bfloat16 or wider, within the bound.
No kernel may reach another device: no remote copies, remote signals or barrier semaphores. Data moves between devices by JAX's collectives and lax.ppermute only.
A program may use at most 128 MiB of HBM per device.

```python
import jax
import jax.numpy as jnp
from jax import lax

ALIGNMENT_WIDTH = 256
FEATURE_SIZE = 32
CZ = 128
HOMOLOG_TOTAL = 256
AMINO_TOTAL = 2048


def draw_genuine_position_indicator(key, part):
    key = jax.random.fold_in(key, 7)
    length = jax.random.randint(key, (), AMINO_TOTAL - AMINO_TOTAL // 4, AMINO_TOTAL)
    return (jnp.arange(AMINO_TOTAL) < length).astype(jnp.int32)


def draw_presence_indicator(key, part):
    key = jax.random.fold_in(key, 11)
    present = jax.random.randint(jax.random.fold_in(key, 1), (HOMOLOG_TOTAL, AMINO_TOTAL), 0, 4)
    present = jnp.minimum(present, 1).astype(jnp.float32)
    level = jax.random.uniform(jax.random.fold_in(key, 2), (HOMOLOG_TOTAL, AMINO_TOTAL), jnp.float32, 0.2, 1.0)
    return (present * level).astype(jnp.bfloat16)


def level_of(rng, dims, shards, low, high):
    factor_of = 1.0
    for dim, parts in shards:
        heights = jax.random.uniform(jax.random.fold_in(jax.random.fold_in(rng, 6), dim), (parts,), jnp.float32, low / len(shards), high / len(shards))
        factor_of = factor_of * jnp.repeat(jnp.exp(heights), dims[dim] // parts).reshape((-1,) + (1,) * (len(dims) - 1 - dim))
    return factor_of


def bell_draw(rng, dims, scale, bound, pieces=(), held_as=jnp.bfloat16):
    loudness = level_of(rng, dims, pieces, -0.22, 0.18) if pieces else 1.0
    values = jax.random.normal(rng, dims, jnp.float32) * scale * loudness
    return jnp.minimum(jnp.maximum(values, -bound), bound).astype(held_as)


def setup_inputs(seed: int = 0) -> dict:
    key_of = jax.random.split(jax.random.key(seed), 12)
    return {
        "alignment_features": bell_draw(key_of[0], (HOMOLOG_TOTAL, AMINO_TOTAL, ALIGNMENT_WIDTH), 1.0, 6.0, ((0, 32), (1, 4))),
        "presence_indicator": draw_presence_indicator(jax.random.fold_in(key_of[11], 71), 0),
        "genuine_position_indicator": draw_genuine_position_indicator(jax.random.fold_in(key_of[11], 71), 0),
        "standardizer_scale": jnp.clip(1.0 + 0.18 * jax.random.normal(key_of[3], (ALIGNMENT_WIDTH,), jnp.float32), 0.1, 1.9),
        "standardizer_offset": bell_draw(key_of[4], (ALIGNMENT_WIDTH,), 0.3, 3.0, (), jnp.float32),
        "first_factor_matrix": bell_draw(key_of[5], (ALIGNMENT_WIDTH, FEATURE_SIZE), ALIGNMENT_WIDTH ** -0.5, 0.375),
        "first_factor_offset": bell_draw(key_of[6], (FEATURE_SIZE,), 0.5, 3.0, (), jnp.float32),
        "second_factor_matrix": bell_draw(key_of[7], (ALIGNMENT_WIDTH, FEATURE_SIZE), ALIGNMENT_WIDTH ** -0.5, 0.375),
        "second_factor_offset": bell_draw(key_of[8], (FEATURE_SIZE,), 0.5, 3.0, (), jnp.float32),
        "final_projection_matrix": bell_draw(key_of[9], (FEATURE_SIZE * FEATURE_SIZE, CZ), (FEATURE_SIZE * FEATURE_SIZE // 64) ** -0.5, 1.5),
        "final_projection_offset": bell_draw(key_of[10], (CZ,), 0.5, 3.0, (), jnp.float32),
    }


def standardize_features(values, standardizer_scale, standardizer_offset):
    values = values.astype(jnp.float32)
    average = lax.optimization_barrier(jnp.mean(values, axis=-1, keepdims=True))
    centred = values - average
    variance = lax.optimization_barrier(jnp.mean(centred * centred, axis=-1, keepdims=True))
    return (centred * lax.rsqrt(variance + 1e-05) * standardizer_scale + standardizer_offset).astype(jnp.bfloat16)

def project(standardized_alignment, weight, shift, kept_mask):
    seqs_here, residues, feature_total = standardized_alignment.shape
    result = jnp.dot(standardized_alignment.reshape(seqs_here * residues, feature_total), weight, preferred_element_type=jnp.float32)
    result = result.reshape(seqs_here, residues, -1)
    return ((result + shift) * kept_mask[..., None].astype(jnp.float32)).astype(jnp.bfloat16)

def reference(alignment_features, presence_indicator, genuine_position_indicator, standardizer_scale, standardizer_offset, first_factor_matrix, first_factor_offset, second_factor_matrix, second_factor_offset, final_projection_matrix, final_projection_offset):
    kept_mask = (presence_indicator.astype(jnp.float32) * genuine_position_indicator[None, :].astype(jnp.float32)).astype(jnp.bfloat16)
    standardized_alignment = standardize_features(alignment_features, standardizer_scale, standardizer_offset)
    left = project(standardized_alignment, first_factor_matrix, first_factor_offset, kept_mask)
    right = project(standardized_alignment, second_factor_matrix, second_factor_offset, kept_mask)
    counts = lax.dot_general(kept_mask, kept_mask, (((0,), (0,)), ((), ())), preferred_element_type=jnp.float32)
    w_grid = final_projection_matrix.reshape(FEATURE_SIZE, FEATURE_SIZE, CZ).astype(jnp.float32)
    right_wide = right.astype(jnp.float32)

    def one_block(offset):
        left_block = lax.dynamic_slice_in_dim(left, offset, 16, 1).astype(jnp.float32)
        outer = jnp.einsum('sic,sje->icje', left_block, right_wide).astype(jnp.bfloat16)
        projected = jnp.einsum('icje,ceh->ijh', outer.astype(jnp.float32), w_grid)
        count_block = lax.dynamic_slice_in_dim(counts, offset, 16, 0)
        return ((projected + final_projection_offset) / jnp.maximum(count_block, 1.0)[..., None]).astype(jnp.bfloat16)
    offsets = (jnp.arange(AMINO_TOTAL // 16) * 16).astype(jnp.int32)
    blocks = lax.map(one_block, offsets)
    return blocks.reshape(AMINO_TOTAL, AMINO_TOTAL, CZ)
```

```python
import functools

import jax
import jax.numpy as jnp
from jax import lax
from jax.experimental import pallas as pl
from jax.experimental.pallas import tpu as pltpu
from jax.sharding import Mesh, PartitionSpec as P

F32 = jnp.float32
BF16 = jnp.bfloat16
ZN, XN, CN, YN = 4, 4, 2, 4
SEQ = 8
CHAN = 256
FEAT = 32
COLS = 512
CB = 128
NB = COLS // CB
ROWS = 64
RW = (FEAT + 1) * CB
LW = (FEAT + 2) * ROWS
OUT = 128
MIB = 2**20


def prepare_kernel(rep_ref, x_ref, pres_ref, gen_ref, sc_ref, of_ref, w_ref, b_ref, r_ref, l_ref, scr):
    kept = (pres_ref[...].astype(F32) * gen_ref[...].astype(F32)).astype(BF16).astype(F32)
    scale = sc_ref[...]
    offset = of_ref[...]
    w = w_ref[...]
    bias = b_ref[...]
    for s in range(SEQ):
        v = x_ref[s].astype(F32)
        centred = v - jnp.mean(v, axis=-1, keepdims=True)
        var = jnp.mean(centred * centred, axis=-1, keepdims=True)
        normed = (centred * lax.rsqrt(var + 1e-05) * scale + offset).astype(BF16)
        p = lax.dot_general(w, normed, (((1,), (1,)), ((), ())), preferred_element_type=F32)
        scr[s * 64 : (s + 1) * 64, :] = (p + bias) * kept[s : s + 1, :]
    for e in range(FEAT):
        r_ref[0, :, e * CB : (e + 1) * CB] = scr[pl.ds(FEAT + e, SEQ, stride=64), :].astype(BF16)
    r_ref[0, :, FEAT * CB :] = kept.astype(BF16)
    for pair in range(FEAT // 2 + 1):
        if pair < FEAT // 2:
            a = scr[pl.ds(2 * pair, SEQ, stride=64), :]
            b = scr[pl.ds(2 * pair + 1, SEQ, stride=64), :]
        else:
            a = kept
            b = jnp.zeros_like(kept)
        for d in range(2):
            both = jnp.concatenate([a[:, d * 64 : (d + 1) * 64], b[:, d * 64 : (d + 1) * 64]], axis=1)
            l_ref[d, :, pair * 128 : (pair + 1) * 128] = both.astype(BF16)


def prepare(rep, x, pres, gen, scale, offset, w, bias):
    return pl.pallas_call(
        prepare_kernel,
        grid_spec=pltpu.PrefetchScalarGridSpec(
            num_scalar_prefetch=1,
            grid=(NB,),
            in_specs=[
                pl.BlockSpec((SEQ, CB, CHAN), lambda q, rep: (0, q, 0)),
                pl.BlockSpec((SEQ, CB), lambda q, rep: (0, q)),
                pl.BlockSpec((1, CB), lambda q, rep: (0, rep[0] * NB + q)),
                pl.BlockSpec((1, CHAN), lambda q, rep: (0, 0)),
                pl.BlockSpec((1, CHAN), lambda q, rep: (0, 0)),
                pl.BlockSpec((2 * FEAT, CHAN), lambda q, rep: (0, 0)),
                pl.BlockSpec((2 * FEAT, 1), lambda q, rep: (0, 0)),
            ],
            out_specs=[
                pl.BlockSpec((1, SEQ, RW), lambda q, rep: (q, 0, 0)),
                pl.BlockSpec((2, SEQ, LW), lambda q, rep: (q, 0, 0)),
            ],
            scratch_shapes=[pltpu.VMEM((SEQ * 64, CB), F32)],
        ),
        out_shape=[
            jax.ShapeDtypeStruct((NB, SEQ, RW), BF16),
            jax.ShapeDtypeStruct((2 * NB, SEQ, LW), BF16),
        ],
        compiler_params=pltpu.CompilerParams(vmem_limit_bytes=32 * MIB),
        cost_estimate=pl.CostEstimate(flops=140_000_000, bytes_accessed=3 * MIB, transcendentals=4096),
        name="prepare",
    )(rep, x, pres, gen, scale, offset, w, bias)


def left_kernel(l_ref, lt_ref, kl_ref, scr):
    for h in range(2):
        half = slice(h * 128, (h + 1) * 128)
        scr[...] = l_ref[half, :].astype(F32).T
        for i in range(ROWS):
            lt_ref[i * FEAT : (i + 1) * FEAT, half] = scr[pl.ds(i, FEAT, stride=ROWS), :].astype(BF16)
        kl_ref[:, half] = scr[FEAT * ROWS : (FEAT + 1) * ROWS, :].astype(BF16)


def arrange_left(l):
    return pl.pallas_call(
        left_kernel,
        out_shape=[
            jax.ShapeDtypeStruct((ROWS * FEAT, 256), BF16),
            jax.ShapeDtypeStruct((ROWS, 256), BF16),
        ],
        scratch_shapes=[pltpu.VMEM((LW, 128), F32)],
        compiler_params=pltpu.CompilerParams(vmem_limit_bytes=32 * MIB),
        cost_estimate=pl.CostEstimate(flops=1_000_000, bytes_accessed=2 * MIB, transcendentals=0),
        name="arrange_left",
    )(l)


def pair_kernel(ib, first, q_ref, lt_ref, kl_ref, r_ref, w_ref, b_ref, *rest):
    o_ref, scr, rcp = rest[-3:]
    step = pl.program_id(0)

    @pl.when(step == 0)
    def _():
        counts = jnp.dot(kl_ref[...], r_ref[:, FEAT * CB :], preferred_element_type=F32)
        rcp[...] = 1.0 / jnp.maximum(counts, 1.0)

    o = jnp.dot(lt_ref[...], r_ref[:, : FEAT * CB], preferred_element_type=F32).astype(BF16)
    for i in range(ib):
        for e in range(FEAT):
            scr[e * FEAT : (e + 1) * FEAT, i * CB : (i + 1) * CB] = o[i * FEAT : (i + 1) * FEAT, e * CB : (e + 1) * CB]
    p = jnp.dot(w_ref[...], scr[...], preferred_element_type=F32)
    for i in range(ib):
        scale = rcp[pl.ds(step * ib + i, 1), :]
        o_ref[i] = ((p[:, i * CB : (i + 1) * CB] + b_ref[...]) * scale).T.astype(BF16)


def pair_block(q, lt, kl, r, w, bias, out, ib=16):
    specs = [
        pl.BlockSpec((ib * FEAT, 256), lambda i, q: (i, 0)),
        pl.BlockSpec((ROWS, 256), lambda i, q: (0, 0)),
        pl.BlockSpec((256, RW), lambda i, q: (0, 0)),
        pl.BlockSpec((OUT, FEAT * FEAT), lambda i, q: (0, 0)),
        pl.BlockSpec((OUT, 1), lambda i, q: (0, 0)),
    ]
    args = [q, lt, kl, r, w, bias]
    aliases = {}
    if out is not None:
        specs.append(pl.BlockSpec(memory_space=pl.ANY))
        args.append(out)
        aliases = {6: 0}
    return pl.pallas_call(
        functools.partial(pair_kernel, ib, out is None),
        grid_spec=pltpu.PrefetchScalarGridSpec(
            num_scalar_prefetch=1,
            grid=(ROWS // ib,),
            in_specs=specs,
            out_specs=pl.BlockSpec((ib, CB, OUT), lambda i, q: (i, q[0], 0)),
            scratch_shapes=[
                pltpu.VMEM((FEAT * FEAT, ib * CB), BF16),
                pltpu.VMEM((ROWS, CB), F32),
            ],
        ),
        out_shape=jax.ShapeDtypeStruct((ROWS, COLS, OUT), BF16),
        input_output_aliases=aliases,
        compiler_params=pltpu.CompilerParams(vmem_limit_bytes=48 * MIB),
        cost_estimate=pl.CostEstimate(
            flops=2 * ROWS * CB * FEAT * FEAT * (256 + OUT), bytes_accessed=6 * MIB, transcendentals=0
        ),
        name="pair_block",
    )(*args)


def shift(v, axis, by):
    return lax.ppermute(v, axis, [(i, (i + by) % 4) for i in range(4)])


def gather_chips(v):
    return lax.all_gather(v, ("z", "x"), axis=0, tiled=True)


def per_device(x, pres, gen, scale, offset, w1, b1, w2, b2, wf, bf):
    core = lax.axis_index("core")
    rep = lax.axis_index("rep").astype(jnp.int32).reshape(1)
    w = jnp.concatenate([w1, w2], axis=1).T
    bias = jnp.concatenate([b1, b2]).reshape(2 * FEAT, 1)
    wt = jnp.transpose(wf.reshape(FEAT, FEAT, OUT), (2, 1, 0)).reshape(OUT, FEAT * FEAT)
    r, l = prepare(
        rep, x, pres, gen.reshape(1, -1), scale.reshape(1, -1), offset.reshape(1, -1), w, bias
    )
    l = lax.ppermute(l, ("z", "rep"), [(z * 4 + y, y * 4 + z) for z in range(4) for y in range(4)])
    l = lax.all_to_all(l, ("x", "core"), split_axis=0, concat_axis=0, tiled=True)
    l = lax.all_gather(l.reshape(XN * CN * SEQ, LW), "rep", axis=0, tiled=True)
    lt, kl = arrange_left(l)
    r = r.reshape(CN, 2, SEQ, RW)
    r = lax.all_to_all(r, "core", split_axis=0, concat_axis=2, tiled=True).reshape(2, CN * SEQ, RW)
    own = [gather_chips(r[k]) for k in range(2)]
    other = [lax.ppermute(v, "core", [(0, 1), (1, 0)]) for v in own]
    out = None
    bf = bf.reshape(OUT, 1)
    for c, rs in ((core, own), (1 - core, other)):
        for k in range(2):
            q = (c * 2 + k).astype(jnp.int32).reshape(1)
            out = pair_block(q, lt, kl, rs[k], wt, bf, out)
    return out


def solution(mesh):
    grid = Mesh(mesh.devices.reshape(ZN, XN, CN, YN), ("z", "x", "core", "rep"))
    dap = ("z", "x", "core")
    in_specs = (P(dap, "rep", None), P(dap, "rep"), P(), P(), P(), P(), P(), P(), P(), P(), P())
    return jax.shard_map(
        per_device, mesh=grid, in_specs=in_specs, out_specs=P(dap, "rep", None), check_vma=False
    )
```

```python
import functools

import jax
import jax.numpy as jnp
from jax import lax
from jax.experimental import pallas as pl
from jax.experimental.pallas import tpu as pltpu
from jax.sharding import Mesh, PartitionSpec as P

F32 = jnp.float32
BF16 = jnp.bfloat16
ZN, XN, CN, YN = 4, 4, 2, 4
SEQ = 8
CHAN = 256
FEAT = 32
COLS = 512
CB = 128
NB = COLS // CB
ROWS = 64
HALF = FEAT // 2
RW = (HALF + 1) * CB
LW = (FEAT + 2) * ROWS
SW = 4 * RW + XN * LW
OUT = 128
RING = (0, -1, 1, 2)
MIB = 2**20


def prepare_kernel(
    rep_ref, x_ref, pres_ref, gen_ref, sc_ref, of_ref, w1_ref, b1_ref, w2_ref, b2_ref, keep_ref, send_ref, scr, w_scr, b_scr
):
    q = pl.program_id(0)

    @pl.when(q == 0)
    def _():
        w_scr[:FEAT, :] = w1_ref[...]
        w_scr[FEAT:, :] = w2_ref[...]
        b_scr[:FEAT, :] = jnp.broadcast_to(b1_ref[...], (CB, FEAT)).T
        b_scr[FEAT:, :] = jnp.broadcast_to(b2_ref[...], (CB, FEAT)).T

    kept = (pres_ref[...].astype(F32) * gen_ref[...].astype(F32)).astype(BF16).astype(F32)
    scale = sc_ref[...]
    offset = of_ref[...]
    w = w_scr[...]
    bias = b_scr[...]
    for s in range(SEQ):
        v = x_ref[s].astype(F32)
        centred = v - jnp.mean(v, axis=-1, keepdims=True)
        var = jnp.mean(centred * centred, axis=-1, keepdims=True)
        normed = (centred * lax.rsqrt(var + 1e-05) * scale + offset).astype(BF16)
        p = lax.dot_general(w, normed, (((1,), (1,)), ((), ())), preferred_element_type=F32)
        scr[s * 64 : (s + 1) * 64, :] = (p + bias) * kept[s : s + 1, :]
    core = lax.axis_index("core")

    def put_right(ref):
        for half in range(2):
            base = (half * 2 + lax.rem(q, 2)) * RW
            for e in range(HALF + 1):
                v = scr[pl.ds(FEAT + half * HALF + e, SEQ, stride=64), :] if e < HALF else kept
                ref[:, pl.ds(pl.multiple_of(base + e * CB, CB), CB)] = v.astype(BF16)

    pl.when(q // 2 == core)(lambda: put_right(keep_ref))
    pl.when(q // 2 != core)(lambda: put_right(send_ref))

    def put_left(refs):
        for pair in range(FEAT // 2 + 1):
            if pair < FEAT // 2:
                a = scr[pl.ds(2 * pair, SEQ, stride=64), :]
                b = scr[pl.ds(2 * pair + 1, SEQ, stride=64), :]
            else:
                a = kept
                b = jnp.zeros_like(kept)
            for d, ref in enumerate(refs):
                both = jnp.concatenate([a[:, d * 64 : (d + 1) * 64], b[:, d * 64 : (d + 1) * 64]], axis=1)
                at = pl.multiple_of(4 * RW + q * LW + pair * 128, 128)
                ref[:, pl.ds(at, 128)] = both.astype(BF16)

    pl.when(core == 0)(lambda: put_left((keep_ref, send_ref)))
    pl.when(core == 1)(lambda: put_left((send_ref, keep_ref)))


def prepare(rep, x, pres, gen, scale, offset, w1, b1, w2, b2):
    whole = lambda *shape: pl.BlockSpec(shape, lambda q, rep: (0, 0))
    return pl.pallas_call(
        prepare_kernel,
        grid_spec=pltpu.PrefetchScalarGridSpec(
            num_scalar_prefetch=1,
            grid=(NB,),
            in_specs=[
                pl.BlockSpec((SEQ, CB, CHAN), lambda q, rep: (0, q, 0)),
                pl.BlockSpec((SEQ, CB), lambda q, rep: (0, q)),
                pl.BlockSpec((1, CB), lambda q, rep: (0, rep[0] * NB + q)),
                whole(1, CHAN),
                whole(1, CHAN),
                whole(FEAT, CHAN),
                whole(1, FEAT),
                whole(FEAT, CHAN),
                whole(1, FEAT),
            ],
            out_specs=[pl.BlockSpec((SEQ, SW), lambda q, rep: (0, 0))] * 2,
            scratch_shapes=[
                pltpu.VMEM((SEQ * 64, CB), F32),
                pltpu.VMEM((2 * FEAT, CHAN), BF16),
                pltpu.VMEM((2 * FEAT, CB), F32),
            ],
        ),
        out_shape=[jax.ShapeDtypeStruct((SEQ, SW), BF16)] * 2,
        compiler_params=pltpu.CompilerParams(vmem_limit_bytes=60 * MIB),
        cost_estimate=pl.CostEstimate(flops=140_000_000, bytes_accessed=3 * MIB, transcendentals=4096),
        name="prepare",
    )(rep, x, pres, gen, scale, offset, w1, b1, w2, b2)


def split_kernel(keep_ref, got_ref, l_ref, first_ref, second_ref, *x_refs):
    core, x = lax.axis_index("core"), lax.axis_index("x")

    def both(lanes):
        keep, got = keep_ref[:, lanes].astype(F32), got_ref[:, lanes].astype(F32)
        rows = [jnp.where(core == 0, keep, got), jnp.where(core == 0, got, keep)]
        return jnp.concatenate(rows, axis=0).astype(BF16)

    first = both(slice(0, 2 * RW))
    first_ref[...] = first
    second_ref[...] = both(slice(2 * RW, 4 * RW))
    for away, ref in zip(RING, (l_ref,) + x_refs):
        left = both(pl.ds(pl.multiple_of(4 * RW + lax.rem(x - away + 4, 4) * LW, 128), LW))
        if away == 0:
            ref[...] = left
        else:
            ref[:, : 2 * RW] = first
            ref[:, 2 * RW :] = left


def split(keep, got):
    return pl.pallas_call(
        split_kernel,
        out_shape=[jax.ShapeDtypeStruct((16, n), BF16) for n in (LW, 2 * RW, 2 * RW) + (2 * RW + LW,) * 3],
        compiler_params=pltpu.CompilerParams(vmem_limit_bytes=16 * MIB),
        cost_estimate=pl.CostEstimate(flops=0, bytes_accessed=MIB, transcendentals=0),
        name="split",
    )(keep, got)


def near_kernel(l_ref, first_ref, second_ref, *refs):
    xs, zs, outs = (first_ref,) + refs[:3], (second_ref,) + refs[3:6], refs[6:]
    z, x = lax.axis_index("z"), lax.axis_index("x")
    for n, away in enumerate(RING):
        at = pl.ds(pl.multiple_of(lax.rem(x + away + 4, 4) * 16, 16), 16)
        outs[0][at, :] = xs[n][:, : 2 * RW]
        outs[2][at, :] = xs[n][:, 2 * RW :] if n else l_ref[...]
        at = pl.ds(pl.multiple_of(lax.rem(z + away + 4, 4) * 16, 16), 16)
        outs[1][at, :] = zs[n][...]


def join_near(l, first, second, xs, zs):
    return pl.pallas_call(
        near_kernel,
        out_shape=[jax.ShapeDtypeStruct((64, n), BF16) for n in (2 * RW, 2 * RW, LW)],
        compiler_params=pltpu.CompilerParams(vmem_limit_bytes=16 * MIB),
        cost_estimate=pl.CostEstimate(flops=0, bytes_accessed=2 * MIB, transcendentals=0),
        name="join_near",
    )(l, first, second, *xs, *zs)


def far_kernel(after_ref, *refs):
    z, x = lax.axis_index("z"), lax.axis_index("x")
    for half, at in ((0, z), (1, x)):
        mine, before, behind, across0, across1 = refs[half * 5 : half * 5 + 5]
        out = refs[10 + half]
        rows = [pl.ds(pl.multiple_of(lax.rem(at + away + 4, 4) * 64, 64), 64) for away in RING]
        out[rows[0], :] = mine[...]
        out[rows[1], :] = before[...]
        out[rows[2], :] = behind[...]
        out[rows[3], :RW] = across0[...]
        out[rows[3], RW:] = across1[...]


def join_far(pieces, after):
    return pl.pallas_call(
        far_kernel,
        in_specs=[pl.BlockSpec(memory_space=pl.ANY)] + [pl.BlockSpec(memory_space=pltpu.VMEM)] * 10,
        out_shape=[jax.ShapeDtypeStruct((256, 2 * RW), BF16)] * 2,
        compiler_params=pltpu.CompilerParams(vmem_limit_bytes=24 * MIB),
        cost_estimate=pl.CostEstimate(flops=0, bytes_accessed=8 * MIB, transcendentals=0),
        name="join_far",
    )(after, *pieces)


def left_kernel(l0_ref, l1_ref, l2_ref, l3_ref, wf_ref, bf_ref, lt_ref, kl_ref, wt_ref, bt_ref, l_ref, mix, scr, w_scr):
    for m, ref in enumerate((l0_ref, l1_ref, l2_ref, l3_ref)):
        l_ref[m * 64 : (m + 1) * 64, :] = ref[...]
    y = lax.axis_index("rep")
    place = lambda away: jnp.where(away == 0, 0, jnp.where(away == 3, 1, away + 1))
    for order in range(2):
        for n in range(ZN * XN):
            z, x = (n % ZN, n // ZN) if order else (n // XN, n % XN)
            source = place(lax.rem(z - y + 4, 4)) * 64 + x * 16
            mix[n * 16 : (n + 1) * 16, :] = l_ref[pl.ds(pl.multiple_of(source, 16), 16), :]
        for h in range(2):
            half = slice(h * 128, (h + 1) * 128)
            scr[...] = mix[half, :].astype(F32).T
            for i in range(ROWS):
                lt_ref[order, i * FEAT : (i + 1) * FEAT, half] = scr[pl.ds(i, FEAT, stride=ROWS), :].astype(BF16)
            if order == 0:
                kl_ref[:, half] = scr[FEAT * ROWS : (FEAT + 1) * ROWS, :].astype(BF16)
    w_scr[...] = wf_ref[...].astype(F32)
    for e in range(0, FEAT, 4):
        four = [w_scr[pl.ds(e + k, FEAT, stride=FEAT), :] for k in range(4)]
        wt_ref[:, e * FEAT : (e + 4) * FEAT] = jnp.concatenate(four, axis=0).T.astype(BF16)
    bt_ref[...] = jnp.broadcast_to(bf_ref[...], (OUT, OUT)).T


def arrange_left(pieces, wf, bf):
    return pl.pallas_call(
        left_kernel,
        out_shape=[
            jax.ShapeDtypeStruct((2, ROWS * FEAT, 256), BF16),
            jax.ShapeDtypeStruct((ROWS, 256), BF16),
            jax.ShapeDtypeStruct((OUT, FEAT * FEAT), BF16),
            jax.ShapeDtypeStruct((OUT, OUT), F32),
        ],
        scratch_shapes=[
            pltpu.VMEM((256, LW), BF16),
            pltpu.VMEM((256, LW), BF16),
            pltpu.VMEM((LW, 128), F32),
            pltpu.VMEM((FEAT * FEAT, OUT), F32),
        ],
        compiler_params=pltpu.CompilerParams(vmem_limit_bytes=32 * MIB),
        cost_estimate=pl.CostEstimate(flops=1_000_000, bytes_accessed=3 * MIB, transcendentals=0),
        name="arrange_left",
    )(*pieces, wf, bf)


def pair_kernel(ib, q_ref, lt_ref, kl_ref, r0_ref, r1_ref, w_ref, b_ref, *rest):
    o_ref, scr, rcp = rest[-3:]
    step = pl.program_id(1)

    @pl.when(step == 0)
    def _():
        counts = jnp.dot(kl_ref[...], r0_ref[:, HALF * CB :], preferred_element_type=F32)
        rcp[...] = 1.0 / jnp.maximum(counts, 1.0)

    for half, r_ref in enumerate((r0_ref, r1_ref)):
        o = jnp.dot(lt_ref[half], r_ref[:, : HALF * CB], preferred_element_type=F32).astype(BF16)
        for i in range(ib):
            for e in range(HALF):
                row = (half * HALF + e) * FEAT
                scr[row : row + FEAT, i * CB : (i + 1) * CB] = o[i * FEAT : (i + 1) * FEAT, e * CB : (e + 1) * CB]
    p = jnp.dot(w_ref[...], scr[...], preferred_element_type=F32)
    for i in range(ib):
        scale = rcp[pl.ds(step * ib + i, 1), :]
        o_ref[i] = ((p[:, i * CB : (i + 1) * CB] + b_ref[...]) * scale).T.astype(BF16)


def pair_block(core, lt, kl, r, w, bias, out, ib=64):
    specs = [
        pl.BlockSpec((2, ib * FEAT, 256), lambda k, i, core: (0, i, 0)),
        pl.BlockSpec((ROWS, 256), lambda k, i, core: (0, 0)),
        pl.BlockSpec((256, RW), lambda k, i, core: (0, k)),
        pl.BlockSpec((256, RW), lambda k, i, core: (0, k)),
        pl.BlockSpec((OUT, FEAT * FEAT), lambda k, i, core: (0, 0)),
        pl.BlockSpec((OUT, OUT), lambda k, i, core: (0, 0)),
    ]
    args = [core, lt, kl, *r, w, bias]
    aliases = {}
    if out is not None:
        specs.append(pl.BlockSpec(memory_space=pl.ANY))
        args.append(out)
        aliases = {7: 0}
    return pl.pallas_call(
        functools.partial(pair_kernel, ib),
        grid_spec=pltpu.PrefetchScalarGridSpec(
            num_scalar_prefetch=1,
            grid=(2, ROWS // ib),
            in_specs=specs,
            out_specs=pl.BlockSpec((ib, CB, OUT), lambda k, i, core: (i, core[0] * 2 + k, 0)),
            scratch_shapes=[
                pltpu.VMEM((FEAT * FEAT, ib * CB), BF16),
                pltpu.VMEM((ROWS, CB), F32),
            ],
        ),
        out_shape=jax.ShapeDtypeStruct((ROWS, COLS, OUT), BF16),
        input_output_aliases=aliases,
        compiler_params=pltpu.CompilerParams(vmem_limit_bytes=40 * MIB),
        cost_estimate=pl.CostEstimate(
            flops=4 * ROWS * CB * FEAT * FEAT * (256 + OUT), bytes_accessed=12 * MIB, transcendentals=0
        ),
        name="pair_block",
    )(*args)


def shift(v, axis, by):
    return lax.ppermute(v, axis, [(i, (i + by) % 4) for i in range(4)])


def ring(v, axis):
    return [v] + [shift(v, axis, -away) for away in RING[1:]]


def ring_onward(v, before, behind, axis):
    return [v, before, behind, shift(before[:, :RW], axis, 1), shift(behind[:, RW:], axis, -1)]


def per_device(x, pres, gen, scale, offset, w1, b1, w2, b2, wf, bf):
    core = lax.axis_index("core")
    rep = lax.axis_index("rep").astype(jnp.int32).reshape(1)
    keep, send = prepare(
        rep,
        x,
        pres,
        gen.reshape(1, -1),
        scale.reshape(1, -1),
        offset.reshape(1, -1),
        w1.T,
        b1.reshape(1, -1),
        w2.T,
        b2.reshape(1, -1),
    )
    swap = lambda v: lax.ppermute(v, "core", [(0, 1), (1, 0)])
    l, first, second, *xs = split(keep, swap(send))
    xs = [shift(v, "x", -away) for v, away in zip(xs, RING[1:])]
    near0, near1, l = join_near(l, first, second, xs, ring(second, "z")[1:])
    l = lax.ppermute(l, ("z", "rep"), [(z * 4 + y, y * 4 + z) for z in range(4) for y in range(4)])
    sides0 = [shift(near0, "z", 1), shift(near0, "z", -1)]
    sides1 = [shift(near1, "x", 1), shift(near1, "x", -1)]
    l = lax.optimization_barrier((l, *sides0, *sides1))[0]
    lt, kl, wt, bt = arrange_left(ring(l, "rep"), wf, bf.reshape(1, -1))
    own = join_far(ring_onward(near0, *sides0, "z") + ring_onward(near1, *sides1, "x"), kl)
    other = [swap(v) for v in own]
    out = pair_block(core.astype(jnp.int32).reshape(1), lt, kl, own, wt, bt, None)
    return pair_block((1 - core).astype(jnp.int32).reshape(1), lt, kl, other, wt, bt, out)


def solution(mesh):
    grid = Mesh(mesh.devices.reshape(ZN, XN, CN, YN), ("z", "x", "core", "rep"))
    dap = ("z", "x", "core")
    in_specs = (P(dap, "rep", None), P(dap, "rep"), P(), P(), P(), P(), P(), P(), P(), P(), P())
    return jax.shard_map(
        per_device, mesh=grid, in_specs=in_specs, out_specs=P(dap, "rep", None), check_vma=False
    )
```

```python
import functools

import jax
import jax.numpy as jnp
from jax import lax
from jax.experimental import pallas as pl
from jax.experimental.pallas import tpu as pltpu
from jax.sharding import Mesh, PartitionSpec as P

F32 = jnp.float32
BF16 = jnp.bfloat16
ZN, XN, CN, YN = 4, 4, 2, 4
SEQ = 8
CHAN = 256
FEAT = 32
COLS = 512
CB = 128
NB = COLS // CB
ROWS = 64
HALF = FEAT // 2
RW = (HALF + 1) * CB
LW = (FEAT + 2) * ROWS
SW = 4 * RW + XN * LW
OUT = 128
RING = (0, -1, 1, 2)
MIB = 2**20


def prepare_kernel(
    rep_ref, x_ref, pres_ref, gen_ref, sc_ref, of_ref, w1_ref, b1_ref, w2_ref, b2_ref, keep_ref, send_ref, scr, w_scr, b_scr
):
    q = pl.program_id(0)

    @pl.when(q == 0)
    def _():
        w_scr[:FEAT, :] = w1_ref[...]
        w_scr[FEAT:, :] = w2_ref[...]
        b_scr[:FEAT, :] = jnp.broadcast_to(b1_ref[...], (CB, FEAT)).T
        b_scr[FEAT:, :] = jnp.broadcast_to(b2_ref[...], (CB, FEAT)).T

    kept = (pres_ref[...].astype(F32) * gen_ref[...].astype(F32)).astype(BF16).astype(F32)
    scale = sc_ref[...]
    offset = of_ref[...]
    w = w_scr[...]
    bias = b_scr[...]
    for s in range(SEQ):
        v = x_ref[s].astype(F32)
        centred = v - jnp.mean(v, axis=-1, keepdims=True)
        var = jnp.mean(centred * centred, axis=-1, keepdims=True)
        normed = (centred * lax.rsqrt(var + 1e-05) * scale + offset).astype(BF16)
        p = lax.dot_general(w, normed, (((1,), (1,)), ((), ())), preferred_element_type=F32)
        scr[s * 64 : (s + 1) * 64, :] = (p + bias) * kept[s : s + 1, :]
    core = lax.axis_index("core")

    def put_right(ref):
        for half in range(2):
            base = (half * 2 + lax.rem(q, 2)) * RW
            for e in range(HALF + 1):
                v = scr[pl.ds(FEAT + half * HALF + e, SEQ, stride=64), :] if e < HALF else kept
                ref[:, pl.ds(pl.multiple_of(base + e * CB, CB), CB)] = v.astype(BF16)

    pl.when(q // 2 == core)(lambda: put_right(keep_ref))
    pl.when(q // 2 != core)(lambda: put_right(send_ref))

    def put_left(refs):
        for pair in range(FEAT // 2 + 1):
            if pair < FEAT // 2:
                a = scr[pl.ds(2 * pair, SEQ, stride=64), :]
                b = scr[pl.ds(2 * pair + 1, SEQ, stride=64), :]
            else:
                a = kept
                b = jnp.zeros_like(kept)
            for d, ref in enumerate(refs):
                both = jnp.concatenate([a[:, d * 64 : (d + 1) * 64], b[:, d * 64 : (d + 1) * 64]], axis=1)
                at = pl.multiple_of(4 * RW + q * LW + pair * 128, 128)
                ref[:, pl.ds(at, 128)] = both.astype(BF16)

    pl.when(core == 0)(lambda: put_left((keep_ref, send_ref)))
    pl.when(core == 1)(lambda: put_left((send_ref, keep_ref)))


def prepare(rep, x, pres, gen, scale, offset, w1, b1, w2, b2):
    whole = lambda *shape: pl.BlockSpec(shape, lambda q, rep: (0, 0))
    return pl.pallas_call(
        prepare_kernel,
        grid_spec=pltpu.PrefetchScalarGridSpec(
            num_scalar_prefetch=1,
            grid=(NB,),
            in_specs=[
                pl.BlockSpec((SEQ, CB, CHAN), lambda q, rep: (0, q, 0)),
                pl.BlockSpec((SEQ, CB), lambda q, rep: (0, q)),
                pl.BlockSpec((1, CB), lambda q, rep: (0, rep[0] * NB + q)),
                whole(1, CHAN),
                whole(1, CHAN),
                whole(FEAT, CHAN),
                whole(1, FEAT),
                whole(FEAT, CHAN),
                whole(1, FEAT),
            ],
            out_specs=[pl.BlockSpec((SEQ, SW), lambda q, rep: (0, 0))] * 2,
            scratch_shapes=[
                pltpu.VMEM((SEQ * 64, CB), F32),
                pltpu.VMEM((2 * FEAT, CHAN), BF16),
                pltpu.VMEM((2 * FEAT, CB), F32),
            ],
        ),
        out_shape=[jax.ShapeDtypeStruct((SEQ, SW), BF16)] * 2,
        compiler_params=pltpu.CompilerParams(vmem_limit_bytes=60 * MIB),
        cost_estimate=pl.CostEstimate(flops=140_000_000, bytes_accessed=3 * MIB, transcendentals=4096),
        name="prepare",
    )(rep, x, pres, gen, scale, offset, w1, b1, w2, b2)


def split_kernel(keep_ref, got_ref, l_ref, first_ref, second_ref, *x_refs):
    core, x = lax.axis_index("core"), lax.axis_index("x")

    def both(lanes):
        keep, got = keep_ref[:, lanes].astype(F32), got_ref[:, lanes].astype(F32)
        rows = [jnp.where(core == 0, keep, got), jnp.where(core == 0, got, keep)]
        return jnp.concatenate(rows, axis=0).astype(BF16)

    first = both(slice(0, 2 * RW))
    first_ref[...] = first
    second_ref[...] = both(slice(2 * RW, 4 * RW))
    for away, ref in zip(RING, (l_ref,) + x_refs):
        left = both(pl.ds(pl.multiple_of(4 * RW + lax.rem(x - away + 4, 4) * LW, 128), LW))
        if away == 0:
            ref[...] = left
        else:
            ref[:, : 2 * RW] = first
            ref[:, 2 * RW :] = left


def split(keep, got):
    return pl.pallas_call(
        split_kernel,
        out_shape=[jax.ShapeDtypeStruct((16, n), BF16) for n in (LW, 2 * RW, 2 * RW) + (2 * RW + LW,) * 3],
        compiler_params=pltpu.CompilerParams(vmem_limit_bytes=16 * MIB),
        cost_estimate=pl.CostEstimate(flops=0, bytes_accessed=MIB, transcendentals=0),
        name="split",
    )(keep, got)


def near_kernel(l_ref, first_ref, second_ref, *refs):
    xs, zs, outs = (first_ref,) + refs[:3], (second_ref,) + refs[3:6], refs[6:]
    z, x = lax.axis_index("z"), lax.axis_index("x")
    for n, away in enumerate(RING):
        at = pl.ds(pl.multiple_of(lax.rem(x + away + 4, 4) * 16, 16), 16)
        outs[0][at, :] = xs[n][:, : 2 * RW]
        outs[2][at, :] = xs[n][:, 2 * RW :] if n else l_ref[...]
        at = pl.ds(pl.multiple_of(lax.rem(z + away + 4, 4) * 16, 16), 16)
        outs[1][at, :] = zs[n][...]


def join_near(l, first, second, xs, zs):
    return pl.pallas_call(
        near_kernel,
        out_shape=[jax.ShapeDtypeStruct((64, n), BF16) for n in (2 * RW, 2 * RW, LW)],
        compiler_params=pltpu.CompilerParams(vmem_limit_bytes=16 * MIB),
        cost_estimate=pl.CostEstimate(flops=0, bytes_accessed=2 * MIB, transcendentals=0),
        name="join_near",
    )(l, first, second, *xs, *zs)


def far_kernel(after_ref, *refs):
    z, x = lax.axis_index("z"), lax.axis_index("x")
    for half, at in ((0, z), (1, x)):
        mine, before, behind, across0, across1 = refs[half * 5 : half * 5 + 5]
        out = refs[10 + half]
        rows = [pl.ds(pl.multiple_of(lax.rem(at + away + 4, 4) * 64, 64), 64) for away in RING]
        out[rows[0], :] = mine[...]
        out[rows[1], :] = before[...]
        out[rows[2], :] = behind[...]
        out[rows[3], :RW] = across0[...]
        out[rows[3], RW:] = across1[...]


def join_far(pieces, after):
    return pl.pallas_call(
        far_kernel,
        in_specs=[pl.BlockSpec(memory_space=pl.ANY)] + [pl.BlockSpec(memory_space=pltpu.VMEM)] * 10,
        out_shape=[jax.ShapeDtypeStruct((256, 2 * RW), BF16)] * 2,
        compiler_params=pltpu.CompilerParams(vmem_limit_bytes=24 * MIB),
        cost_estimate=pl.CostEstimate(flops=0, bytes_accessed=8 * MIB, transcendentals=0),
        name="join_far",
    )(after, *pieces)


def left_kernel(l0_ref, l1_ref, l2_ref, l3_ref, lt_ref, kl_ref, l_ref, mix, scr):
    for m, ref in enumerate((l0_ref, l1_ref, l2_ref, l3_ref)):
        l_ref[m * 64 : (m + 1) * 64, :] = ref[...]
    y = lax.axis_index("rep")
    place = lambda away: jnp.where(away == 0, 0, jnp.where(away == 3, 1, away + 1))
    for order in range(2):
        for n in range(ZN * XN):
            z, x = (n % ZN, n // ZN) if order else (n // XN, n % XN)
            source = place(lax.rem(z - y + 4, 4)) * 64 + x * 16
            mix[n * 16 : (n + 1) * 16, :] = l_ref[pl.ds(pl.multiple_of(source, 16), 16), :]
        for h in range(2):
            half = slice(h * 128, (h + 1) * 128)
            scr[...] = mix[half, :].astype(F32).T
            for i in range(ROWS):
                lt_ref[order, i * FEAT : (i + 1) * FEAT, half] = scr[pl.ds(i, FEAT, stride=ROWS), :].astype(BF16)
            if order == 0:
                kl_ref[:, half] = scr[FEAT * ROWS : (FEAT + 1) * ROWS, :].astype(BF16)


def arrange_left(pieces):
    return pl.pallas_call(
        left_kernel,
        out_shape=[
            jax.ShapeDtypeStruct((2, ROWS * FEAT, 256), BF16),
            jax.ShapeDtypeStruct((ROWS, 256), BF16),
        ],
        scratch_shapes=[
            pltpu.VMEM((256, LW), BF16),
            pltpu.VMEM((256, LW), BF16),
            pltpu.VMEM((LW, 128), F32),
        ],
        compiler_params=pltpu.CompilerParams(vmem_limit_bytes=32 * MIB),
        cost_estimate=pl.CostEstimate(flops=1_000_000, bytes_accessed=3 * MIB, transcendentals=0),
        name="arrange_left",
    )(*pieces)


def weights_kernel(after_ref, wf_ref, bf_ref, wt_ref, bt_ref, w_scr):
    w_scr[...] = wf_ref[...].astype(F32)
    for e in range(0, FEAT, 4):
        four = [w_scr[pl.ds(e + k, FEAT, stride=FEAT), :] for k in range(4)]
        wt_ref[:, e * FEAT : (e + 4) * FEAT] = jnp.concatenate(four, axis=0).T.astype(BF16)
    bt_ref[...] = jnp.broadcast_to(bf_ref[...], (OUT, OUT)).T


def arrange_weights(wf, bf, after):
    return pl.pallas_call(
        weights_kernel,
        in_specs=[pl.BlockSpec(memory_space=pl.ANY)] + [pl.BlockSpec(memory_space=pltpu.VMEM)] * 2,
        out_shape=[jax.ShapeDtypeStruct((OUT, FEAT * FEAT), BF16), jax.ShapeDtypeStruct((OUT, OUT), F32)],
        scratch_shapes=[pltpu.VMEM((FEAT * FEAT, OUT), F32)],
        compiler_params=pltpu.CompilerParams(vmem_limit_bytes=16 * MIB),
        cost_estimate=pl.CostEstimate(flops=1_000_000, bytes_accessed=MIB, transcendentals=0),
        name="arrange_weights",
    )(after, wf, bf)


def pair_kernel(ib, q_ref, lt_ref, kl_ref, r0_ref, r1_ref, w_ref, b_ref, *rest):
    o_ref, scr, rcp = rest[-3:]
    step = pl.program_id(1)

    @pl.when(step == 0)
    def _():
        counts = jnp.dot(kl_ref[...], r0_ref[:, HALF * CB :], preferred_element_type=F32)
        rcp[...] = 1.0 / jnp.maximum(counts, 1.0)

    for half, r_ref in enumerate((r0_ref, r1_ref)):
        o = jnp.dot(lt_ref[half], r_ref[:, : HALF * CB], preferred_element_type=F32).astype(BF16)
        for i in range(ib):
            for e in range(HALF):
                row = (half * HALF + e) * FEAT
                scr[row : row + FEAT, i * CB : (i + 1) * CB] = o[i * FEAT : (i + 1) * FEAT, e * CB : (e + 1) * CB]
    p = jnp.dot(w_ref[...], scr[...], preferred_element_type=F32)
    for i in range(ib):
        scale = rcp[pl.ds(step * ib + i, 1), :]
        o_ref[i] = ((p[:, i * CB : (i + 1) * CB] + b_ref[...]) * scale).T.astype(BF16)


def pair_block(core, lt, kl, r, w, bias, out, ib=64):
    specs = [
        pl.BlockSpec((2, ib * FEAT, 256), lambda k, i, core: (0, i, 0)),
        pl.BlockSpec((ROWS, 256), lambda k, i, core: (0, 0)),
        pl.BlockSpec((256, RW), lambda k, i, core: (0, k)),
        pl.BlockSpec((256, RW), lambda k, i, core: (0, k)),
        pl.BlockSpec((OUT, FEAT * FEAT), lambda k, i, core: (0, 0)),
        pl.BlockSpec((OUT, OUT), lambda k, i, core: (0, 0)),
    ]
    args = [core, lt, kl, *r, w, bias]
    aliases = {}
    if out is not None:
        specs.append(pl.BlockSpec(memory_space=pl.ANY))
        args.append(out)
        aliases = {7: 0}
    return pl.pallas_call(
        functools.partial(pair_kernel, ib),
        grid_spec=pltpu.PrefetchScalarGridSpec(
            num_scalar_prefetch=1,
            grid=(2, ROWS // ib),
            in_specs=specs,
            out_specs=pl.BlockSpec((ib, CB, OUT), lambda k, i, core: (i, core[0] * 2 + k, 0)),
            scratch_shapes=[
                pltpu.VMEM((FEAT * FEAT, ib * CB), BF16),
                pltpu.VMEM((ROWS, CB), F32),
            ],
        ),
        out_shape=jax.ShapeDtypeStruct((ROWS, COLS, OUT), BF16),
        input_output_aliases=aliases,
        compiler_params=pltpu.CompilerParams(vmem_limit_bytes=40 * MIB),
        cost_estimate=pl.CostEstimate(
            flops=4 * ROWS * CB * FEAT * FEAT * (256 + OUT), bytes_accessed=12 * MIB, transcendentals=0
        ),
        name="pair_block",
    )(*args)


def shift(v, axis, by):
    return lax.ppermute(v, axis, [(i, (i + by) % 4) for i in range(4)])


def ring(v, axis):
    return [v] + [shift(v, axis, -away) for away in RING[1:]]


def ring_onward(v, before, behind, axis):
    return [v, before, behind, shift(before[:, :RW], axis, 1), shift(behind[:, RW:], axis, -1)]


def per_device(x, pres, gen, scale, offset, w1, b1, w2, b2, wf, bf):
    core = lax.axis_index("core")
    rep = lax.axis_index("rep").astype(jnp.int32).reshape(1)
    keep, send = prepare(
        rep,
        x,
        pres,
        gen.reshape(1, -1),
        scale.reshape(1, -1),
        offset.reshape(1, -1),
        w1.T,
        b1.reshape(1, -1),
        w2.T,
        b2.reshape(1, -1),
    )
    swap = lambda v: lax.ppermute(v, "core", [(0, 1), (1, 0)])
    l, first, second, *xs = split(keep, swap(send))
    xs = [shift(v, "x", -away) for v, away in zip(xs, RING[1:])]
    near0, near1, l = join_near(l, first, second, xs, ring(second, "z")[1:])
    l = lax.ppermute(l, ("z", "rep"), [(z * 4 + y, y * 4 + z) for z in range(4) for y in range(4)])
    near0, l = lax.optimization_barrier((near0, l))
    sides0 = [shift(near0, "z", 1), shift(near0, "z", -1)]
    sides1 = [shift(near1, "x", 1), shift(near1, "x", -1)]
    wt, bt = arrange_weights(wf, bf.reshape(1, -1), near0)
    lt, kl = arrange_left(ring(l, "rep"))
    own = join_far(ring_onward(near0, *sides0, "z") + ring_onward(near1, *sides1, "x"), kl)
    other = [swap(v) for v in own]
    out = pair_block(core.astype(jnp.int32).reshape(1), lt, kl, own, wt, bt, None)
    return pair_block((1 - core).astype(jnp.int32).reshape(1), lt, kl, other, wt, bt, out)


def solution(mesh):
    grid = Mesh(mesh.devices.reshape(ZN, XN, CN, YN), ("z", "x", "core", "rep"))
    dap = ("z", "x", "core")
    in_specs = (P(dap, "rep", None), P(dap, "rep"), P(), P(), P(), P(), P(), P(), P(), P(), P())
    return jax.shard_map(
        per_device, mesh=grid, in_specs=in_specs, out_specs=P(dap, "rep", None), check_vma=False
    )
```
